32 devices in a mesh: clips: 2 (over x), tile: 16 (over z, y, core).
Axes of the slice: x: 2, y: 2, z: 4, core: 2. Of those that a mesh axis runs over, the one named last changes fastest.
Arguments:
- latents: bfloat16 [12, 16, 8, 160], P('clips', 'tile'), parts along dimension 0, may hold values from -18 to 18
- w_in: bfloat16 [432, 384], replicated, may hold values from -0.3125 to 0.3125
- b_in: float32 [384], replicated, may hold values from -3 to 3
- gain_mid: float32 [384], replicated, may hold values from 0.1 to 1.9
- w_mid: bfloat16 [10368, 384], replicated, may hold values from -0.0625 to 0.0625
- b_mid: float32 [384], replicated, may hold values from -3 to 3
- w_up: bfloat16 [3456, 192], replicated, may hold values from -0.109375 to 0.109375
- b_up: float32 [192], replicated, may hold values from -3 to 3
Outputs:
- decoded: bfloat16 [8, 16, 16, 3840], P('clips', 'tile'), parts along dimension 0
The draws below stay inside these ranges and needn't reach their ends.
There are 2 independent parts, one for each index of `clips`. The reference program is written for one: setup_inputs(seed, part) draws one part's arguments, and reference() takes and returns one part's arrays. A program takes and returns all parts, laid end to end along the dimension named above; an argument that names none is the same for every part. Nothing has to cross between parts.
All inputs are finite; a program needn't handle non-finite values.
Results may differ from the reference program's by a relative error of at most 0.006.
Values may be sent and summed in bfloat16 or wider, within the bound.
A program may use at most 128 MiB of HBM per device.

```python
import jax
import jax.numpy as jnp
from jax import lax

C_LAT = 16
C_MID = 384
C_UP = 192
FR = 4
CACHE = 2
GC = 16
TH = 8
TW = 10
FT = 6
GR = 1
HGT = 8
WID = 160
N_TILE = 16


def draw_latents(key, part):
    first_key = jax.random.fold_in(key, 0)
    row_index = (jnp.arange(N_TILE) // GC)[:, None] * TH + jnp.arange(TH)[None, :]
    levels = 3.0 ** (row_index.astype(jnp.float32) / max(HGT - 1, 1))
    full_shape = (FT, N_TILE, TH, TW * C_LAT)
    sample = jnp.clip(jax.random.normal(first_key, full_shape, jnp.float32), -6.0, 6.0)
    return (sample * levels[None, :, :, None]).astype(jnp.bfloat16)


def scatter_about(own_key, extent, spread, limit, kind=jnp.bfloat16):
    return jnp.clip(spread * jax.random.normal(own_key, extent, jnp.float32), -limit, limit).astype(kind)


def setup_inputs(seed: int = 0, part: int = 0) -> dict:
    key_of = jax.random.split(jax.random.key(seed), 9)
    part_keys = jax.random.split(jax.random.fold_in(key_of[8], part), 9)
    return {
        "latents": draw_latents(jax.random.fold_in(jax.random.fold_in(key_of[8], part), 71), part),
        "w_in": scatter_about(key_of[1], (27 * C_LAT, C_MID), (27 * C_LAT) ** -0.5, 0.3125),
        "b_in": scatter_about(key_of[2], (C_MID,), 0.5, 3.0, jnp.float32),
        "gain_mid": jnp.clip(1.0 + 0.18 * jax.random.normal(key_of[3], (C_MID,), jnp.float32), 0.1, 1.9),
        "w_mid": scatter_about(key_of[4], (27 * C_MID, C_MID), (27 * C_MID) ** -0.5, 0.0625),
        "b_mid": scatter_about(key_of[5], (C_MID,), 0.5, 3.0, jnp.float32),
        "w_up": scatter_about(key_of[6], (9 * C_MID, C_UP), (9 * C_MID) ** -0.5, 0.109375),
        "b_up": scatter_about(key_of[7], (C_UP,), 0.5, 3.0, jnp.float32),
    }


def to_image(latents):
    shaped = latents.reshape(FT, GR, GC, TH, TW, C_LAT)
    return shaped.transpose(0, 1, 3, 2, 4, 5).reshape(FT, HGT, WID, C_LAT)

def from_image(image):
    shaped = image.reshape(FR, GR, 2 * TH, GC, 2 * TW, C_UP)
    return shaped.transpose(0, 1, 3, 2, 4, 5).reshape(FR, N_TILE, 2 * TH, 2 * TW * C_UP)

def causal_conv(field, weight, in_chan, out_chan):
    kernel = weight.reshape(3, 3, 3, in_chan, out_chan)
    result = lax.conv_general_dilated(field[None], kernel, (1, 1, 1), ((2, 0), (1, 1), (1, 1)), dimension_numbers=('NDHWC', 'DHWIO', 'NDHWC'), preferred_element_type=jnp.float32)
    return result[0]

def rms_norm_act(hidden, gain_mid):
    values = hidden.astype(jnp.float32)
    inverse = lax.rsqrt(lax.optimization_barrier(jnp.mean(values * values, axis=-1, keepdims=True)) + 1e-06)
    return jax.nn.silu(values * inverse * gain_mid).astype(jnp.bfloat16)

def reference(latents, w_in, b_in, gain_mid, w_mid, b_mid, w_up, b_up):
    image = to_image(latents)
    hidden = (causal_conv(image, w_in, C_LAT, C_MID) + b_in).astype(jnp.bfloat16)
    normed = rms_norm_act(hidden, gain_mid)
    residual = (hidden.astype(jnp.float32) + causal_conv(normed, w_mid, C_MID, C_MID) + b_mid).astype(jnp.bfloat16)
    last = residual[CACHE:]
    grown = jnp.repeat(jnp.repeat(last, 2, axis=1), 2, axis=2)
    kernel = w_up.reshape(3, 3, C_MID, C_UP)
    output = lax.conv_general_dilated(grown, kernel, (1, 1), ((1, 1), (1, 1)), dimension_numbers=('NHWC', 'HWIO', 'NHWC'), preferred_element_type=jnp.float32)
    return from_image((output + b_up).astype(jnp.bfloat16))
```

```python
import functools

import jax
import jax.numpy as jnp
from jax import lax
from jax.experimental import pallas as pl
from jax.experimental.pallas import tpu as pltpu
from jax.sharding import PartitionSpec as P

CACHE = 2
GC = 16
BF = jnp.bfloat16
F32 = jnp.float32
MESH = pl.DeviceIdType.MESH


def shift_rows(v, b):
    if b == 1:
        return v
    rows = v.shape[1]
    row = lax.broadcasted_iota(jnp.int32, v.shape, 1)
    moved = pltpu.roll(v, 1 if b == 0 else rows - 1, 1)
    return jnp.where(row == (0 if b == 0 else rows - 1), 0.0, moved)


def kernel(
    sizes, lat, w_in, b_in, gain, w_mid, b_mid, w_up, b_up, out,
    xin, xrecv, xs, win_v, wpad, wmid_v, wup_v, wc, bias, lhs, hacc, hbuf, nab, acc, rb, outs,
    send_sem, recv_sem, in_sem, up_sem, mid_sem,
):
    frames, th, tw, cl, cm, cu, gr, rows, off = sizes
    keep = frames - CACHE
    nw, rw = tw + 4, tw + 2
    me = lax.axis_index("tile")
    col, grow = lax.rem(me, GC), lax.div(me, GC)

    in_copy = pltpu.make_async_copy(w_in, win_v, in_sem)
    up_copy = pltpu.make_async_copy(w_up, wup_v, up_sem)
    part = 9 * cm
    mid_copies = [
        pltpu.make_async_copy(
            w_mid.at[pl.ds(a * part, part), :], wmid_v.at[pl.ds(a * part, part), :], mid_sem.at[a]
        )
        for a in range(3)
    ]

    steps = [(0, -1), (0, 1)]
    if gr > 1:
        steps += [(-1, -1), (-1, 0), (-1, 1), (1, -1), (1, 0), (1, 1)]

    def there(step):
        dr, dc = step
        ok = (col + dc >= 0) & (col + dc < GC)
        if dr:
            ok = ok & (grow + dr >= 0) & (grow + dr < gr)
        return ok

    barrier = pltpu.get_barrier_semaphore()
    for step in steps:
        @pl.when(there(step))
        def _():
            pl.semaphore_signal(
                barrier, inc=1, device_id={"tile": me + step[0] * GC + step[1]}, device_id_type=MESH
            )

    in_copy.start()
    up_copy.start()
    for copy in mid_copies:
        copy.start()

    xin[...] = jnp.zeros_like(xin)
    xin[:, 0 : tw * cl] = lat[...]
    for k, step in enumerate(steps):
        @pl.when(jnp.logical_not(there(step)))
        def _():
            xrecv[k] = jnp.zeros(xin.shape, BF)

    pl.semaphore_wait(barrier, sum(there(step).astype(jnp.int32) for step in steps))

    def copy_to(k, slot):
        dr, dc = steps[k]
        return pltpu.make_async_remote_copy(
            src_ref=xin,
            dst_ref=xrecv.at[slot],
            send_sem=send_sem.at[k],
            recv_sem=recv_sem.at[slot],
            device_id={"tile": me + dr * GC + dc},
            device_id_type=MESH,
        )

    for k, (dr, dc) in enumerate(steps):
        @pl.when(there((dr, dc)))
        def _():
            copy_to(k, steps.index((-dr, -dc))).start()

    wpad[...] = jnp.zeros_like(wpad)
    in_copy.wait()
    for g in range(9):
        wpad[g * 128 : g * 128 + 3 * cl, :] = win_v[g * 3 * cl : (g + 1) * 3 * cl, :]

    wide = 2 * cu - 128
    bias[...] = jnp.zeros_like(bias)
    bias[0:1, 0:cu] = b_up[...].reshape(1, cu)
    first = bias[...]
    second = pltpu.roll(first, wide - cu, 1)
    bias3 = jnp.concatenate(
        [first[0:1, :128], first[0:1, 128:] + second[0:1, :128], second[0:1, 128:]], axis=1
    )

    up_copy.wait()
    blk = 16
    for phase in range(4):
        spare = pl.ds(0, wide - cu) if phase % 2 else pl.ds(cu, wide - cu)
        wc[phase, spare, :] = jnp.zeros((wide - cu, 4 * cm), BF)

    @pl.loop(0, cu // blk)
    def _(t):
        base = pl.multiple_of(t * blk, blk)
        for c in range(0, cm, 128):
            w = [
                [
                    wup_v[
                        pl.ds(base, blk), (3 * b + e) * cm + c : (3 * b + e) * cm + c + 128
                    ].astype(F32)
                    for e in range(3)
                ]
                for b in range(3)
            ]
            for py in range(2):
                two = [w[0][e] + w[1][e] if py else w[1][e] + w[2][e] for e in range(3)]
                for ro, (e0, e1, e2) in enumerate([two, w[2]] if py else [w[0], two]):
                    for px in range(2):
                        for co, v in enumerate([e0 + e1, e2] if px else [e0, e1 + e2]):
                            at = (2 * ro + co) * cm + c
                            row = pl.multiple_of(base + px * (wide - cu), blk)
                            wc[2 * py + px, pl.ds(row, blk), at : at + 128] = v.astype(BF)

    xs[...] = jnp.zeros_like(xs)
    for k in range(len(steps)):
        @pl.when(there(steps[k]))
        def _():
            copy_to(k, k).wait_recv()

    def image_rows(dr):
        mine = xin[...] if dr == 0 else xrecv[steps.index((dr, 0))]
        left, right = xrecv[steps.index((dr, -1))], xrecv[steps.index((dr, 1))]
        mine, left, right = mine.astype(F32), left.astype(F32), right.astype(F32)
        width = xin.shape[1]
        lane = lax.broadcasted_iota(jnp.int32, mine.shape, 1)
        m = 3 * cl
        whole = jnp.where(
            lane < m,
            pltpu.roll(left, width - (tw - 3) * cl, 1),
            jnp.where(lane < m + tw * cl, pltpu.roll(mine, m, 1), pltpu.roll(right, m + tw * cl, 1)),
        )
        return whole.reshape(frames, th, width)

    xs[2:, off : off + th, :] = image_rows(0)
    if gr > 1:
        xs[2:, 0:3, :] = image_rows(-1)[:, th - 3 :, :]
        xs[2:, off + th : off + th + 3, :] = image_rows(1)[:, 0:3, :]

    fr = frames * rows
    field = xs[...]
    for b in range(3):
        moved = shift_rows(field, b)
        for j in range(nw):
            width = xin.shape[1]
            turned = pltpu.roll(moved, width - j * cl, 2) if j else moved
            for a in range(3):
                g = 3 * a + b
                lhs[j * fr : (j + 1) * fr, g * 128 : (g + 1) * 128] = (
                    turned[a : a + frames, :, :128].reshape(fr, 128).astype(BF)
                )
    hacc[...] = jnp.dot(lhs[...], wpad[...], preferred_element_type=F32)

    def inside(v, j, margin):
        place = col * tw + j - margin
        ok = (place >= 0) & (place < GC * tw)
        if gr > 1:
            row = grow * th + lax.broadcasted_iota(jnp.int32, v.shape, 1) - off
            ok = ok & (row >= 0) & (row < gr * th)
        return jnp.where(ok, v, 0.0)

    kr = keep * rows

    @pl.loop(0, nw)
    def _(j):
        at = pl.multiple_of(j * fr, fr)
        hb = (hacc[pl.ds(at, fr), :] + b_in[...].reshape(1, cm)).astype(BF)
        hbuf[pl.ds(at, fr), :] = hb
        v = hb.astype(F32)
        v = v * lax.rsqrt(jnp.mean(v * v, axis=-1, keepdims=True) + 1e-06) * gain[...].reshape(1, cm)
        half = 0.5 * v
        n = half + half * jnp.tanh(half)
        n = inside(n.reshape(frames, rows, cm), j, 2)
        for b in range(3):
            moved = shift_rows(n, b)
            for a in range(3):
                nab[3 * a + b, pl.ds(pl.multiple_of(j * kr, kr), kr), :] = (
                    moved[a : a + keep].reshape(kr, cm).astype(BF)
                )

    for a in range(3):
        mid_copies[a].wait()
        taps = jnp.concatenate(
            [nab[3 * a + b, e * kr : (e + rw) * kr, :] for b in range(3) for e in range(3)], axis=1
        )
        total = jnp.dot(
            taps, wmid_v[a * part : (a + 1) * part, :], preferred_element_type=F32
        )
        acc[...] = total if a == 0 else acc[...] + total

    @pl.loop(0, rw)
    def _(j):
        at = pl.multiple_of(j * kr, kr)
        own = pl.ds(pl.multiple_of((j + 1) * fr + CACHE * rows, CACHE * rows), kr)
        r = hbuf[own, :].astype(F32) + acc[pl.ds(at, kr), :] + b_mid[...].reshape(1, cm)
        r = inside(r.astype(BF).astype(F32).reshape(keep, rows, cm), j, 1)
        for b in range(3):
            rb[b, pl.ds(at, kr), :] = shift_rows(r, b).reshape(kr, cm).astype(BF)

    strips = 2 * cu // 128
    for py in range(2):
        o = []
        for px in range(2):
            taps = jnp.concatenate(
                [
                    rb[py + ro, (px + co) * kr : (px + co + tw) * kr, :]
                    for ro in range(2)
                    for co in range(2)
                ],
                axis=1,
            )
            o.append(
                lax.dot_general(
                    taps, wc[2 * py + px], (((1,), (1,)), ((), ())), preferred_element_type=F32
                )
            )
        joined = (
            jnp.concatenate([o[0][:, :128], o[0][:, 128:] + o[1][:, :128], o[1][:, 128:]], axis=1)
            + bias3
        )
        for j in range(tw):
            for f in range(keep):
                at = j * kr + f * rows + off
                for c in range(strips):
                    outs[j * strips + c, pl.ds(f * 2 * th + py, th, stride=2), :] = joined[
                        at : at + th, c * 128 : (c + 1) * 128
                    ]
    for f in range(keep):
        for c in range(strips * tw):
            out[f, 0, :, c * 128 : (c + 1) * 128] = outs[c, f * 2 * th : (f + 1) * 2 * th, :].astype(BF)

    for k in range(len(steps)):
        @pl.when(there(steps[k]))
        def _():
            copy_to(k, k).wait_send()


def body(latents, w_in, b_in, gain_mid, w_mid, b_mid, w_up, b_up):
    frames, _, th, packed = latents.shape
    cl = w_in.shape[0] // 27
    tw = packed // cl
    cm, cu = w_in.shape[1], w_up.shape[1]
    gr = lax.axis_size("tile") // GC
    rows, off = (th, 0) if gr == 1 else (2 * th, 3)
    keep = frames - CACHE
    nw, rw = tw + 4, tw + 2
    width = (tw + 6) * cl
    sizes = (frames, th, tw, cl, cm, cu, gr, rows, off)
    near = 2 if gr == 1 else 8
    vm = pl.BlockSpec(memory_space=pltpu.VMEM)
    hbm = pl.BlockSpec(memory_space=pl.ANY)
    flops = 2 * keep * rows * rw * 27 * cm * cm
    return pl.pallas_call(
        functools.partial(kernel, sizes),
        out_shape=jax.ShapeDtypeStruct((keep, 1, 2 * th, 2 * tw * cu), BF),
        in_specs=[vm, hbm, vm, vm, hbm, vm, hbm, vm],
        out_specs=vm,
        scratch_shapes=[
            pltpu.VMEM((frames * th, width), BF),
            pltpu.VMEM((near, frames * th, width), BF),
            pltpu.VMEM((frames + 2, rows, width), F32),
            pltpu.VMEM(w_in.shape, BF),
            pltpu.VMEM((9 * 128, cm), BF),
            pltpu.VMEM(w_mid.shape, BF),
            pltpu.VMEM((cu, 9 * cm), BF),
            pltpu.VMEM((4, 2 * cu - 128, 4 * cm), BF),
            pltpu.VMEM((8, 2 * cu - 128), F32),
            pltpu.VMEM((nw * frames * rows, 9 * 128), BF),
            pltpu.VMEM((nw * frames * rows, cm), F32),
            pltpu.VMEM((nw * frames * rows, cm), BF),
            pltpu.VMEM((9, nw * keep * rows, cm), BF),
            pltpu.VMEM((rw * keep * rows, cm), F32),
            pltpu.VMEM((3, rw * keep * rows, cm), BF),
            pltpu.VMEM((2 * tw * cu // 128, keep * 2 * th, 128), F32),
            pltpu.SemaphoreType.DMA((near,)),
            pltpu.SemaphoreType.DMA((near,)),
            pltpu.SemaphoreType.DMA,
            pltpu.SemaphoreType.DMA,
            pltpu.SemaphoreType.DMA((3,)),
        ],
        compiler_params=pltpu.CompilerParams(
            collective_id=0, has_side_effects=True, vmem_limit_bytes=56 * 2**20
        ),
        cost_estimate=pl.CostEstimate(flops=flops, bytes_accessed=10**7, transcendentals=0),
    )(
        latents.reshape(frames * th, packed),
        w_in,
        b_in,
        gain_mid,
        w_mid,
        b_mid,
        w_up.T,
        b_up,
    )


def solution(mesh):
    placed = (P("clips", "tile", None, None), P(), P(), P(), P(), P(), P(), P())
    return jax.shard_map(
        body, mesh=mesh, in_specs=placed, out_specs=P("clips", "tile", None, None), check_vma=False
    )
```

```python
import functools

import jax
import jax.numpy as jnp
from jax import lax
from jax.experimental import pallas as pl
from jax.experimental.pallas import tpu as pltpu
from jax.sharding import PartitionSpec as P

CACHE = 2
GC = 16
BF = jnp.bfloat16
F32 = jnp.float32
MESH = pl.DeviceIdType.MESH


def shift_rows(v, b):
    if b == 1:
        return v
    rows = v.shape[1]
    row = lax.broadcasted_iota(jnp.int32, v.shape, 1)
    moved = pltpu.roll(v, 1 if b == 0 else rows - 1, 1)
    return jnp.where(row == (0 if b == 0 else rows - 1), 0.0, moved)


def exchange(sizes, lat, field, xin, xrecv, xs, send_sem, recv_sem):
    frames, th, tw, cl, cm, cu, gr, rows, off = sizes
    me = lax.axis_index("tile")
    col, grow = lax.rem(me, GC), lax.div(me, GC)

    steps = [(0, -1), (0, 1)]
    if gr > 1:
        steps += [(-1, -1), (-1, 0), (-1, 1), (1, -1), (1, 0), (1, 1)]

    def there(step):
        dr, dc = step
        ok = (col + dc >= 0) & (col + dc < GC)
        if dr:
            ok = ok & (grow + dr >= 0) & (grow + dr < gr)
        return ok

    barrier = pltpu.get_barrier_semaphore()
    for step in steps:
        @pl.when(there(step))
        def _():
            pl.semaphore_signal(
                barrier, inc=1, device_id={"tile": me + step[0] * GC + step[1]}, device_id_type=MESH
            )

    xin[...] = jnp.zeros_like(xin)
    xin[:, 0 : tw * cl] = lat[...]
    for k, step in enumerate(steps):
        @pl.when(jnp.logical_not(there(step)))
        def _():
            xrecv[k] = jnp.zeros(xin.shape, BF)

    pl.semaphore_wait(barrier, sum(there(step).astype(jnp.int32) for step in steps))

    def copy_to(k, slot):
        dr, dc = steps[k]
        return pltpu.make_async_remote_copy(
            src_ref=xin,
            dst_ref=xrecv.at[slot],
            send_sem=send_sem.at[k],
            recv_sem=recv_sem.at[slot],
            device_id={"tile": me + dr * GC + dc},
            device_id_type=MESH,
        )

    for k, (dr, dc) in enumerate(steps):
        @pl.when(there((dr, dc)))
        def _():
            copy_to(k, steps.index((-dr, -dc))).start()

    xs[...] = jnp.zeros_like(xs)
    for k in range(len(steps)):
        @pl.when(there(steps[k]))
        def _():
            copy_to(k, k).wait_recv()

    def image_rows(dr):
        mine = xin[...] if dr == 0 else xrecv[steps.index((dr, 0))]
        left, right = xrecv[steps.index((dr, -1))], xrecv[steps.index((dr, 1))]
        mine, left, right = mine.astype(F32), left.astype(F32), right.astype(F32)
        width = xin.shape[1]
        lane = lax.broadcasted_iota(jnp.int32, mine.shape, 1)
        m = 3 * cl
        whole = jnp.where(
            lane < m,
            pltpu.roll(left, width - (tw - 3) * cl, 1),
            jnp.where(lane < m + tw * cl, pltpu.roll(mine, m, 1), pltpu.roll(right, m + tw * cl, 1)),
        )
        return whole.reshape(frames, th, width)

    xs[:, off : off + th, :] = image_rows(0)
    if gr > 1:
        xs[:, 0:3, :] = image_rows(-1)[:, th - 3 :, :]
        xs[:, off + th : off + th + 3, :] = image_rows(1)[:, 0:3, :]

    field[...] = xs[...].reshape(field.shape).astype(BF)

    for k in range(len(steps)):
        @pl.when(there(steps[k]))
        def _():
            copy_to(k, k).wait_send()


def convolve(
    sizes, field, w_in, b_in, gain, w_mid, b_mid, w_up, b_up, out,
    win_v, wpad, wmid_v, wup_v, wc, bias, lhs, hacc, hbuf, nab, acc, rb, outs,
    in_sem, up_sem, mid_sem,
):
    frames, th, tw, cl, cm, cu, gr, rows, off = sizes
    keep = frames - CACHE
    nw, rw = tw + 4, tw + 2
    width = (tw + 6) * cl
    me = lax.axis_index("tile")
    col, grow = lax.rem(me, GC), lax.div(me, GC)

    in_copy = pltpu.make_async_copy(w_in, win_v, in_sem)
    up_copy = pltpu.make_async_copy(w_up, wup_v, up_sem)
    mid_copy = pltpu.make_async_copy(w_mid, wmid_v, mid_sem)

    in_copy.start()
    mid_copy.start()
    up_copy.start()

    fr = frames * rows
    image = jnp.concatenate(
        [jnp.zeros((2, rows, width), F32), field[...].astype(F32).reshape(frames, rows, width)], axis=0
    )
    for b in range(3):
        moved = shift_rows(image, b)
        for j in range(nw):
            turned = pltpu.roll(moved, width - j * cl, 2) if j else moved
            for a in range(3):
                g = 3 * a + b
                lhs[j * fr : (j + 1) * fr, g * 128 : (g + 1) * 128] = (
                    turned[a : a + frames, :, :128].reshape(fr, 128).astype(BF)
                )
    wpad[...] = jnp.zeros_like(wpad)
    in_copy.wait()
    for g in range(9):
        wpad[g * 128 : g * 128 + 3 * cl, :] = win_v[g * 3 * cl : (g + 1) * 3 * cl, :]

    hacc[...] = jnp.dot(lhs[...], wpad[...], preferred_element_type=F32)

    wide = 2 * cu - 128
    bias[...] = jnp.zeros_like(bias)
    bias[0:1, 0:cu] = b_up[...].reshape(1, cu)
    first = bias[...]
    second = pltpu.roll(first, wide - cu, 1)
    bias3 = jnp.concatenate(
        [first[0:1, :128], first[0:1, 128:] + second[0:1, :128], second[0:1, 128:]], axis=1
    )

    def inside(v, j, margin):
        place = col * tw + j - margin
        ok = (place >= 0) & (place < GC * tw)
        if gr > 1:
            row = grow * th + lax.broadcasted_iota(jnp.int32, v.shape, 1) - off
            ok = ok & (row >= 0) & (row < gr * th)
        return jnp.where(ok, v, 0.0)

    kr = keep * rows

    @pl.loop(0, nw, unroll=nw)
    def _(j):
        at = pl.multiple_of(j * fr, fr)
        hb = (hacc[pl.ds(at, fr), :] + b_in[...].reshape(1, cm)).astype(BF)
        hbuf[pl.ds(at, fr), :] = hb
        v = hb.astype(F32)
        v = v * lax.rsqrt(jnp.mean(v * v, axis=-1, keepdims=True) + 1e-06) * gain[...].reshape(1, cm)
        half = 0.5 * v
        n = half + half * jnp.tanh(half)
        n = inside(n.reshape(frames, rows, cm), j, 2)
        for b in range(3):
            moved = shift_rows(n, b)
            for a in range(3):
                nab[3 * a + b, pl.ds(pl.multiple_of(j * kr, kr), kr), :] = (
                    moved[a : a + keep].reshape(kr, cm).astype(BF)
                )

    up_copy.wait()
    blk = 16
    for phase in range(4):
        spare = pl.ds(0, wide - cu) if phase % 2 else pl.ds(cu, wide - cu)
        wc[phase, spare, :] = jnp.zeros((wide - cu, 4 * cm), BF)

    @pl.loop(0, cu // blk)
    def _(t):
        base = pl.multiple_of(t * blk, blk)
        for c in range(0, cm, 128):
            w = [
                [
                    wup_v[
                        pl.ds(base, blk), (3 * b + e) * cm + c : (3 * b + e) * cm + c + 128
                    ].astype(F32)
                    for e in range(3)
                ]
                for b in range(3)
            ]
            for py in range(2):
                two = [w[0][e] + w[1][e] if py else w[1][e] + w[2][e] for e in range(3)]
                for ro, (e0, e1, e2) in enumerate([two, w[2]] if py else [w[0], two]):
                    for px in range(2):
                        for co, v in enumerate([e0 + e1, e2] if px else [e0, e1 + e2]):
                            at = (2 * ro + co) * cm + c
                            row = pl.multiple_of(base + px * (wide - cu), blk)
                            wc[2 * py + px, pl.ds(row, blk), at : at + 128] = v.astype(BF)

    mid_copy.wait()
    taps = jnp.concatenate(
        [nab[i, e * kr : (e + rw) * kr, :] for i in range(9) for e in range(3)], axis=1
    )
    acc[...] = jnp.dot(taps, wmid_v[...], preferred_element_type=F32)

    @pl.loop(0, rw, unroll=rw)
    def _(j):
        at = pl.multiple_of(j * kr, kr)
        own = pl.ds(pl.multiple_of((j + 1) * fr + CACHE * rows, CACHE * rows), kr)
        r = hbuf[own, :].astype(F32) + acc[pl.ds(at, kr), :] + b_mid[...].reshape(1, cm)
        r = inside(r.astype(BF).astype(F32).reshape(keep, rows, cm), j, 1)
        for b in range(3):
            rb[b, pl.ds(at, kr), :] = shift_rows(r, b).reshape(kr, cm).astype(BF)

    strips = 2 * cu // 128
    for py in range(2):
        o = []
        for px in range(2):
            taps = jnp.concatenate(
                [
                    rb[py + ro, (px + co) * kr : (px + co + tw) * kr, :]
                    for ro in range(2)
                    for co in range(2)
                ],
                axis=1,
            )
            o.append(
                lax.dot_general(
                    taps, wc[2 * py + px], (((1,), (1,)), ((), ())), preferred_element_type=F32
                )
            )
        joined = (
            jnp.concatenate([o[0][:, :128], o[0][:, 128:] + o[1][:, :128], o[1][:, 128:]], axis=1)
            + bias3
        )
        for j in range(tw):
            for f in range(keep):
                at = j * kr + f * rows + off
                for c in range(strips):
                    outs[j * strips + c, pl.ds(f * 2 * th + py, th, stride=2), :] = joined[
                        at : at + th, c * 128 : (c + 1) * 128
                    ]
    for f in range(keep):
        for c in range(strips * tw):
            out[f, 0, :, c * 128 : (c + 1) * 128] = outs[c, f * 2 * th : (f + 1) * 2 * th, :].astype(BF)


def body(latents, w_in, b_in, gain_mid, w_mid, b_mid, w_up, b_up):
    frames, _, th, packed = latents.shape
    cl = w_in.shape[0] // 27
    tw = packed // cl
    cm, cu = w_in.shape[1], w_up.shape[1]
    gr = lax.axis_size("tile") // GC
    rows, off = (th, 0) if gr == 1 else (2 * th, 3)
    keep = frames - CACHE
    nw, rw = tw + 4, tw + 2
    width = (tw + 6) * cl
    sizes = (frames, th, tw, cl, cm, cu, gr, rows, off)
    near = 2 if gr == 1 else 8
    vm = pl.BlockSpec(memory_space=pltpu.VMEM)
    hbm = pl.BlockSpec(memory_space=pl.ANY)
    field = pl.pallas_call(
        functools.partial(exchange, sizes),
        out_shape=jax.ShapeDtypeStruct((frames * rows, width), BF),
        in_specs=[vm],
        out_specs=vm,
        scratch_shapes=[
            pltpu.VMEM((frames * th, width), BF),
            pltpu.VMEM((near, frames * th, width), BF),
            pltpu.VMEM((frames, rows, width), F32),
            pltpu.SemaphoreType.DMA((near,)),
            pltpu.SemaphoreType.DMA((near,)),
        ],
        compiler_params=pltpu.CompilerParams(
            collective_id=0, has_side_effects=True, vmem_limit_bytes=4 * 2**20
        ),
        cost_estimate=pl.CostEstimate(flops=10**6, bytes_accessed=10**5, transcendentals=0),
    )(latents.reshape(frames * th, packed))
    flops = 2 * keep * rows * rw * 27 * cm * cm
    return pl.pallas_call(
        functools.partial(convolve, sizes),
        out_shape=jax.ShapeDtypeStruct((keep, 1, 2 * th, 2 * tw * cu), BF),
        in_specs=[vm, hbm, vm, vm, hbm, vm, hbm, vm],
        out_specs=vm,
        scratch_shapes=[
            pltpu.VMEM(w_in.shape, BF),
            pltpu.VMEM((9 * 128, cm), BF),
            pltpu.VMEM(w_mid.shape, BF),
            pltpu.VMEM((cu, 9 * cm), BF),
            pltpu.VMEM((4, 2 * cu - 128, 4 * cm), BF),
            pltpu.VMEM((8, 2 * cu - 128), F32),
            pltpu.VMEM((nw * frames * rows, 9 * 128), BF),
            pltpu.VMEM((nw * frames * rows, cm), F32),
            pltpu.VMEM((nw * frames * rows, cm), BF),
            pltpu.VMEM((9, nw * keep * rows, cm), BF),
            pltpu.VMEM((rw * keep * rows, cm), F32),
            pltpu.VMEM((3, rw * keep * rows, cm), BF),
            pltpu.VMEM((2 * tw * cu // 128, keep * 2 * th, 128), F32),
            pltpu.SemaphoreType.DMA,
            pltpu.SemaphoreType.DMA,
            pltpu.SemaphoreType.DMA,
        ],
        compiler_params=pltpu.CompilerParams(vmem_limit_bytes=40 * 2**20),
        cost_estimate=pl.CostEstimate(flops=flops, bytes_accessed=10**7, transcendentals=0),
    )(field, w_in, b_in, gain_mid, w_mid, b_mid, w_up.T, b_up)


def solution(mesh):
    placed = (P("clips", "tile", None, None), P(), P(), P(), P(), P(), P(), P())
    return jax.shard_map(
        body, mesh=mesh, in_specs=placed, out_specs=P("clips", "tile", None, None), check_vma=False
    )
```

```python
import functools

import jax
import jax.numpy as jnp
from jax import lax
from jax.experimental import pallas as pl
from jax.experimental.pallas import tpu as pltpu
from jax.sharding import PartitionSpec as P

CACHE = 2
GC = 16
BF = jnp.bfloat16
F32 = jnp.float32
MESH = pl.DeviceIdType.MESH


def shift_rows(v, b):
    if b == 1:
        return v
    rows = v.shape[1]
    row = lax.broadcasted_iota(jnp.int32, v.shape, 1)
    moved = pltpu.roll(v, 1 if b == 0 else rows - 1, 1)
    return jnp.where(row == (0 if b == 0 else rows - 1), 0.0, moved)


def kernel(
    sizes, lat, w_in, b_in, gain, w_mid, b_mid, w_up, b_up, out,
    xin, xrecv, xs, win_v, wpad, wmid_v, wup_v, wc, bias, lhs, hacc, hbuf, nab, acc, rb, outs,
    send_sem, recv_sem, in_sem, up_sem, mid_sem,
):
    frames, th, tw, cl, cm, cu, gr, rows, off = sizes
    keep = frames - CACHE
    nw, rw = tw + 4, tw + 2
    me = lax.axis_index("tile")
    col, grow = lax.rem(me, GC), lax.div(me, GC)

    in_copy = pltpu.make_async_copy(w_in, win_v, in_sem)
    up_copy = pltpu.make_async_copy(w_up, wup_v, up_sem)
    mid_copy = pltpu.make_async_copy(w_mid, wmid_v, mid_sem)

    steps = [(0, -1), (0, 1)]
    if gr > 1:
        steps += [(-1, -1), (-1, 0), (-1, 1), (1, -1), (1, 0), (1, 1)]

    def there(step):
        dr, dc = step
        ok = (col + dc >= 0) & (col + dc < GC)
        if dr:
            ok = ok & (grow + dr >= 0) & (grow + dr < gr)
        return ok

    barrier = pltpu.get_barrier_semaphore()
    for step in steps:
        @pl.when(there(step))
        def _():
            pl.semaphore_signal(
                barrier, inc=1, device_id={"tile": me + step[0] * GC + step[1]}, device_id_type=MESH
            )

    in_copy.start()
    up_copy.start()
    mid_copy.start()

    xin[...] = jnp.zeros_like(xin)
    xin[:, 0 : tw * cl] = lat[...]
    for k, step in enumerate(steps):
        @pl.when(jnp.logical_not(there(step)))
        def _():
            xrecv[k] = jnp.zeros(xin.shape, BF)

    pl.semaphore_wait(barrier, sum(there(step).astype(jnp.int32) for step in steps))

    def copy_to(k, slot):
        dr, dc = steps[k]
        return pltpu.make_async_remote_copy(
            src_ref=xin,
            dst_ref=xrecv.at[slot],
            send_sem=send_sem.at[k],
            recv_sem=recv_sem.at[slot],
            device_id={"tile": me + dr * GC + dc},
            device_id_type=MESH,
        )

    for k, (dr, dc) in enumerate(steps):
        @pl.when(there((dr, dc)))
        def _():
            copy_to(k, steps.index((-dr, -dc))).start()

    wpad[...] = jnp.zeros_like(wpad)
    in_copy.wait()
    for g in range(9):
        wpad[g * 128 : g * 128 + 3 * cl, :] = win_v[g * 3 * cl : (g + 1) * 3 * cl, :]

    wide = 2 * cu - 128
    bias[...] = jnp.zeros_like(bias)
    bias[0:1, 0:cu] = b_up[...].reshape(1, cu)
    first = bias[...]
    second = pltpu.roll(first, wide - cu, 1)
    bias3 = jnp.concatenate(
        [first[0:1, :128], first[0:1, 128:] + second[0:1, :128], second[0:1, 128:]], axis=1
    )

    up_copy.wait()
    blk = 16
    for phase in range(4):
        spare = pl.ds(0, wide - cu) if phase % 2 else pl.ds(cu, wide - cu)
        wc[phase, spare, :] = jnp.zeros((wide - cu, 4 * cm), BF)

    @pl.loop(0, cu // blk)
    def _(t):
        base = pl.multiple_of(t * blk, blk)
        for c in range(0, cm, 128):
            w = [
                [
                    wup_v[
                        pl.ds(base, blk), (3 * b + e) * cm + c : (3 * b + e) * cm + c + 128
                    ].astype(F32)
                    for e in range(3)
                ]
                for b in range(3)
            ]
            for py in range(2):
                two = [w[0][e] + w[1][e] if py else w[1][e] + w[2][e] for e in range(3)]
                for ro, (e0, e1, e2) in enumerate([two, w[2]] if py else [w[0], two]):
                    for px in range(2):
                        for co, v in enumerate([e0 + e1, e2] if px else [e0, e1 + e2]):
                            at = (2 * ro + co) * cm + c
                            row = pl.multiple_of(base + px * (wide - cu), blk)
                            wc[2 * py + px, pl.ds(row, blk), at : at + 128] = v.astype(BF)

    xs[...] = jnp.zeros_like(xs)
    for k in range(len(steps)):
        @pl.when(there(steps[k]))
        def _():
            copy_to(k, k).wait_recv()

    def image_rows(dr):
        mine = xin[...] if dr == 0 else xrecv[steps.index((dr, 0))]
        left, right = xrecv[steps.index((dr, -1))], xrecv[steps.index((dr, 1))]
        mine, left, right = mine.astype(F32), left.astype(F32), right.astype(F32)
        width = xin.shape[1]
        lane = lax.broadcasted_iota(jnp.int32, mine.shape, 1)
        m = 3 * cl
        whole = jnp.where(
            lane < m,
            pltpu.roll(left, width - (tw - 3) * cl, 1),
            jnp.where(lane < m + tw * cl, pltpu.roll(mine, m, 1), pltpu.roll(right, m + tw * cl, 1)),
        )
        return whole.reshape(frames, th, width)

    xs[2:, off : off + th, :] = image_rows(0)
    if gr > 1:
        xs[2:, 0:3, :] = image_rows(-1)[:, th - 3 :, :]
        xs[2:, off + th : off + th + 3, :] = image_rows(1)[:, 0:3, :]

    fr = frames * rows
    field = xs[...]
    for b in range(3):
        moved = shift_rows(field, b)
        for j in range(nw):
            width = xin.shape[1]
            turned = pltpu.roll(moved, width - j * cl, 2) if j else moved
            for a in range(3):
                g = 3 * a + b
                lhs[j * fr : (j + 1) * fr, g * 128 : (g + 1) * 128] = (
                    turned[a : a + frames, :, :128].reshape(fr, 128).astype(BF)
                )
    hacc[...] = jnp.dot(lhs[...], wpad[...], preferred_element_type=F32)

    def inside(v, j, margin):
        place = col * tw + j - margin
        ok = (place >= 0) & (place < GC * tw)
        if gr > 1:
            row = grow * th + lax.broadcasted_iota(jnp.int32, v.shape, 1) - off
            ok = ok & (row >= 0) & (row < gr * th)
        return jnp.where(ok, v, 0.0)

    kr = keep * rows

    @pl.loop(0, nw, unroll=nw)
    def _(j):
        at = pl.multiple_of(j * fr, fr)
        hb = (hacc[pl.ds(at, fr), :] + b_in[...].reshape(1, cm)).astype(BF)
        hbuf[pl.ds(at, fr), :] = hb
        v = hb.astype(F32)
        v = v * lax.rsqrt(jnp.mean(v * v, axis=-1, keepdims=True) + 1e-06) * gain[...].reshape(1, cm)
        half = 0.5 * v
        n = half + half * jnp.tanh(half)
        n = inside(n.reshape(frames, rows, cm), j, 2)
        for b in range(3):
            moved = shift_rows(n, b)
            for a in range(3):
                nab[3 * a + b, pl.ds(pl.multiple_of(j * kr, kr), kr), :] = (
                    moved[a : a + keep].reshape(kr, cm).astype(BF)
                )

    mid_copy.wait()
    taps = jnp.concatenate(
        [nab[i, e * kr : (e + rw) * kr, :] for i in range(9) for e in range(3)], axis=1
    )
    acc[...] = jnp.dot(taps, wmid_v[...], preferred_element_type=F32)

    @pl.loop(0, rw, unroll=rw)
    def _(j):
        at = pl.multiple_of(j * kr, kr)
        own = pl.ds(pl.multiple_of((j + 1) * fr + CACHE * rows, CACHE * rows), kr)
        r = hbuf[own, :].astype(F32) + acc[pl.ds(at, kr), :] + b_mid[...].reshape(1, cm)
        r = inside(r.astype(BF).astype(F32).reshape(keep, rows, cm), j, 1)
        for b in range(3):
            rb[b, pl.ds(at, kr), :] = shift_rows(r, b).reshape(kr, cm).astype(BF)

    strips = 2 * cu // 128
    for py in range(2):
        o = []
        for px in range(2):
            taps = jnp.concatenate(
                [
                    rb[py + ro, (px + co) * kr : (px + co + tw) * kr, :]
                    for ro in range(2)
                    for co in range(2)
                ],
                axis=1,
            )
            o.append(
                lax.dot_general(
                    taps, wc[2 * py + px], (((1,), (1,)), ((), ())), preferred_element_type=F32
                )
            )
        joined = (
            jnp.concatenate([o[0][:, :128], o[0][:, 128:] + o[1][:, :128], o[1][:, 128:]], axis=1)
            + bias3
        )
        for j in range(tw):
            for f in range(keep):
                at = j * kr + f * rows + off
                for c in range(strips):
                    outs[j * strips + c, pl.ds(f * 2 * th + py, th, stride=2), :] = joined[
                        at : at + th, c * 128 : (c + 1) * 128
                    ]
    for f in range(keep):
        for c in range(strips * tw):
            out[f, 0, :, c * 128 : (c + 1) * 128] = outs[c, f * 2 * th : (f + 1) * 2 * th, :].astype(BF)

    for k in range(len(steps)):
        @pl.when(there(steps[k]))
        def _():
            copy_to(k, k).wait_send()


def body(latents, w_in, b_in, gain_mid, w_mid, b_mid, w_up, b_up):
    frames, _, th, packed = latents.shape
    cl = w_in.shape[0] // 27
    tw = packed // cl
    cm, cu = w_in.shape[1], w_up.shape[1]
    gr = lax.axis_size("tile") // GC
    rows, off = (th, 0) if gr == 1 else (2 * th, 3)
    keep = frames - CACHE
    nw, rw = tw + 4, tw + 2
    width = (tw + 6) * cl
    sizes = (frames, th, tw, cl, cm, cu, gr, rows, off)
    near = 2 if gr == 1 else 8
    vm = pl.BlockSpec(memory_space=pltpu.VMEM)
    hbm = pl.BlockSpec(memory_space=pl.ANY)
    flops = 2 * keep * rows * rw * 27 * cm * cm
    return pl.pallas_call(
        functools.partial(kernel, sizes),
        out_shape=jax.ShapeDtypeStruct((keep, 1, 2 * th, 2 * tw * cu), BF),
        in_specs=[vm, hbm, vm, vm, hbm, vm, hbm, vm],
        out_specs=vm,
        scratch_shapes=[
            pltpu.VMEM((frames * th, width), BF),
            pltpu.VMEM((near, frames * th, width), BF),
            pltpu.VMEM((frames + 2, rows, width), F32),
            pltpu.VMEM(w_in.shape, BF),
            pltpu.VMEM((9 * 128, cm), BF),
            pltpu.VMEM(w_mid.shape, BF),
            pltpu.VMEM((cu, 9 * cm), BF),
            pltpu.VMEM((4, 2 * cu - 128, 4 * cm), BF),
            pltpu.VMEM((8, 2 * cu - 128), F32),
            pltpu.VMEM((nw * frames * rows, 9 * 128), BF),
            pltpu.VMEM((nw * frames * rows, cm), F32),
            pltpu.VMEM((nw * frames * rows, cm), BF),
            pltpu.VMEM((9, nw * keep * rows, cm), BF),
            pltpu.VMEM((rw * keep * rows, cm), F32),
            pltpu.VMEM((3, rw * keep * rows, cm), BF),
            pltpu.VMEM((2 * tw * cu // 128, keep * 2 * th, 128), F32),
            pltpu.SemaphoreType.DMA((near,)),
            pltpu.SemaphoreType.DMA((near,)),
            pltpu.SemaphoreType.DMA,
            pltpu.SemaphoreType.DMA,
            pltpu.SemaphoreType.DMA,
        ],
        compiler_params=pltpu.CompilerParams(
            collective_id=0, has_side_effects=True, vmem_limit_bytes=56 * 2**20
        ),
        cost_estimate=pl.CostEstimate(flops=flops, bytes_accessed=10**7, transcendentals=0),
    )(
        latents.reshape(frames * th, packed),
        w_in,
        b_in,
        gain_mid,
        w_mid,
        b_mid,
        w_up.T,
        b_up,
    )


def solution(mesh):
    placed = (P("clips", "tile", None, None), P(), P(), P(), P(), P(), P(), P())
    return jax.shard_map(
        body, mesh=mesh, in_specs=placed, out_specs=P("clips", "tile", None, None), check_vma=False
    )
```
